32 devices in a mesh: sx: 8 (over z, core), sy: 4 (over y, x).
Axes of the slice: x: 2, y: 2, z: 4, core: 2. Of those that a mesh axis runs over, the one named last changes fastest.
Arguments:
- features: bfloat16 [64, 128, 512], P(None, 'sx', 'sy'), may hold values from -6 to 6
- enc_weight: bfloat16 [3, 3, 3, 64, 64], replicated, may hold values from -0.15625 to 0.15625
- enc_bias: float32 [64], replicated, may hold values from -3 to 3
- proj_weight: bfloat16 [64, 512], replicated, may hold values from -0.25 to 0.25
- bottle_weight: bfloat16 [3, 3, 3, 512, 512], P(None, None, None, 'sy'), may hold values from -0.0546875 to 0.0546875
- bottle_bias: float32 [512], P('sy'), may hold values from -3 to 3
- out_weight: bfloat16 [512, 64], P('sy'), may hold values from -0.25 to 0.25
- dec_weight: bfloat16 [3, 3, 3, 64, 64], replicated, may hold values from -0.15625 to 0.15625
- dec_bias: float32 [64], replicated, may hold values from -3 to 3
Outputs:
- decoded: bfloat16 [64, 128, 512], P(None, 'sx', 'sy')
The draws below stay inside these ranges and needn't reach their ends.
All inputs are finite; a program needn't handle non-finite values.
Results may differ from the reference program's by a relative error of at most 0.009.
Values may be sent and summed in bfloat16 or wider, within the bound.
A program may use at most 64 MiB of HBM per device.

```python
import jax
import jax.numpy as jnp
from jax import lax

C = 64
CB = 512
POOL = 8
FZ = 16
NX = 128
NY = 32


def steps_of(rng, extent, split, smallest, high):
    loudness = 1.0
    for dim, shards_of in split:
        heights = jax.random.uniform(jax.random.fold_in(jax.random.fold_in(rng, 6), dim), (shards_of,), jnp.float32, smallest / len(split), high / len(split))
        loudness = loudness * jnp.repeat(jnp.exp(heights), extent[dim] // shards_of).reshape((-1,) + (1,) * (len(extent) - 1 - dim))
    return loudness


def scatter_about(stream_key, extent, deviation, reach, split=(), held_as=jnp.bfloat16):
    factor_of = steps_of(stream_key, extent, split, -0.22, 0.18) if split else 1.0
    array = jax.random.normal(stream_key, extent, jnp.float32) * deviation * factor_of
    return jnp.minimum(jnp.maximum(array, -reach), reach).astype(held_as)


def setup_inputs(seed: int = 0) -> dict:
    splits = jax.random.split(jax.random.key(seed), 10)
    return {
        "features": scatter_about(splits[0], (C, NX, NY * FZ), 1.0, 6.0, ((1, 8), (2, 4))),
        "enc_weight": scatter_about(splits[1], (3, 3, 3, C, C), (27 * C) ** -0.5, 0.15625),
        "enc_bias": scatter_about(splits[2], (C,), 0.5, 3.0, (), jnp.float32),
        "proj_weight": scatter_about(splits[3], (C, CB), (9 * C) ** -0.5, 0.25),
        "bottle_weight": scatter_about(splits[4], (3, 3, 3, CB, CB), (27 * CB) ** -0.5, 0.0546875, ((3, 4),)),
        "bottle_bias": scatter_about(splits[5], (CB,), 0.5, 3.0, ((0, 4),), jnp.float32),
        "out_weight": scatter_about(splits[6], (CB, C), CB ** -0.5, 0.25, ((0, 4),)),
        "dec_weight": scatter_about(splits[7], (3, 3, 3, C, C), (27 * C) ** -0.5, 0.15625),
        "dec_bias": scatter_about(splits[8], (C,), 0.5, 3.0, (), jnp.float32),
    }


layout = ("NCDHW", "DHWOI", "NCDHW")


def convolve(field, kernel):
    result = lax.conv_general_dilated(field[None].astype(jnp.float32), kernel.astype(jnp.float32), (1, 1, 1), ((1, 1), (1, 1), (1, 1)), dimension_numbers=layout, precision=lax.Precision.HIGHEST)
    return result[0]


def interpolate(fine_count, fine_first, coarse_count, coarse_first, coarse_total):
    fine_index = fine_first + jnp.arange(fine_count, dtype=jnp.int32)
    coarse_index = coarse_first + jnp.arange(coarse_count, dtype=jnp.int32)
    numerator = 2 * fine_index + 1 - POOL
    low_cell = jnp.floor_divide(numerator, 2 * POOL)
    weight_high = (numerator - 2 * POOL * low_cell).astype(jnp.float32) / jnp.float32(2 * POOL)
    weight_high = jnp.where(low_cell < 0, jnp.float32(0.0), weight_high)
    low_cell = jnp.maximum(low_cell, 0)
    weight_high = jnp.where(low_cell >= coarse_total - 1, jnp.float32(0.0), weight_high)
    low_cell = jnp.minimum(low_cell, coarse_total - 1)
    low_hit = (coarse_index[None, :] == low_cell[:, None]).astype(jnp.float32)
    high_hit = (coarse_index[None, :] == low_cell[:, None] + 1).astype(jnp.float32)
    return (1.0 - weight_high)[:, None] * low_hit + weight_high[:, None] * high_hit


def reference(features, enc_weight, enc_bias, proj_weight, bottle_weight, bottle_bias, out_weight, dec_weight, dec_bias):
    highest = lax.Precision.HIGHEST
    channels, size_x, merged = features.shape
    size_z = FZ
    size_y = merged // size_z
    field = features.reshape(channels, size_x, size_y, size_z)
    encoded = jax.nn.relu(convolve(field, enc_weight) + enc_bias[:, None, None, None]).astype(jnp.bfloat16)
    cells_x, cells_y, cells_z = size_x // POOL, size_y // POOL, size_z // POOL
    pooled = jnp.max(encoded.reshape(channels, cells_x, POOL, cells_y, POOL, cells_z, POOL), axis=(2, 4, 6))
    projected = jnp.einsum("ck,cxyz->kxyz", proj_weight.astype(jnp.float32), pooled.astype(jnp.float32), precision=highest).astype(jnp.bfloat16)
    bottleneck = jax.nn.relu(convolve(projected, bottle_weight) + bottle_bias[:, None, None, None]).astype(jnp.bfloat16)
    lowres = jnp.einsum("kc,kxyz->cxyz", out_weight.astype(jnp.float32), bottleneck.astype(jnp.float32), precision=highest)
    along_x = interpolate(size_x, 0, cells_x, 0, cells_x)
    along_y = interpolate(size_y, 0, cells_y, 0, cells_y)
    along_z = interpolate(size_z, 0, cells_z, 0, cells_z)
    step_one = jnp.einsum("kabc,zc->kabz", lowres, along_z, precision=highest)
    step_two = jnp.einsum("kabz,yb->kayz", step_one, along_y, precision=highest)
    upsampled = jnp.einsum("kayz,xa->kxyz", step_two, along_x, precision=highest)
    joined = (encoded.astype(jnp.float32) + upsampled).astype(jnp.bfloat16)
    decoded = (convolve(joined, dec_weight) + dec_bias[:, None, None, None]).astype(jnp.bfloat16)
    return decoded.reshape(channels, size_x, merged)
```

```python
import functools

import jax
import jax.numpy as jnp
import numpy as np
from jax import lax
from jax.experimental import pallas as pl
from jax.experimental.pallas import tpu as pltpu
from jax.sharding import PartitionSpec as P

POOL = 8
FZ = 16
MESH = pl.DeviceIdType.MESH
BF = jnp.bfloat16
F32 = jnp.float32
SIDES = (-1, 0, 1)


def cell_selector(y_devices):
    outs = 4 * y_devices
    sel = np.zeros((27, outs, 3 * y_devices * 16), np.float32)
    for tap in range(27):
        a, b, c = tap // 9, tap // 3 % 3, tap % 3
        for row in range(outs):
            x, y, z = row // (2 * y_devices) + a - 1, row // 2 % y_devices + b - 1, row % 2 + c - 1
            if 0 <= y < y_devices and 0 <= z < 2:
                side, slot = ((0, 1), (1, 0), (1, 1), (2, 0))[x + 1]
                sel[tap, row, (side * y_devices + y) * 16 + slot * 2 + z] = 1
    return sel.reshape(27 * outs, -1)


def row_of(g, n):
    row = np.zeros(n)
    u = min(max((2 * g - 7) / 16, 0), n - 1)
    lo = int(np.floor(u))
    row[lo] += 1 - (u - lo)
    if lo + 1 < n:
        row[lo + 1] += u - lo
    return row


def plane_weights(y_devices, fine_y):
    total = y_devices * fine_y
    table = np.zeros((y_devices, fine_y + 2, FZ, y_devices, 2), np.float32)
    for s in range(y_devices):
        for y in range(fine_y + 2):
            g = min(max(s * fine_y + y - 1, 0), total - 1)
            table[s, y] = row_of(g, y_devices)[None, :, None] * np.stack([row_of(z, 2) for z in range(FZ)])[:, None, :]
    table = table.reshape(y_devices, (fine_y + 2) * FZ, -1)
    return np.concatenate([table] * 3, axis=2)


def dot_nt(a, b):
    return lax.dot_general(a, b, (((1,), (1,)), ((), ())), preferred_element_type=F32)


def dot(a, b):
    return jnp.dot(a, b, preferred_element_type=F32)


def arrange(w_ref, wm):
    ch = w_ref.shape[1]
    zero = jnp.zeros((ch, ch), BF)
    for bc in range(9):
        w0, w1, w2 = (w_ref[a * 9 + bc] for a in range(3))
        cols = pl.ds(bc * 2 * ch, 2 * ch)
        for n, (left, right) in enumerate(((w1, w2), (w0, w1), (zero, w0), (w2, zero))):
            wm[pl.ds(n * ch, ch), cols] = jnp.concatenate([left, right], axis=1)


def z_taps(value, z):
    rows = value.shape[0]
    below = jnp.where(z == 0, 0.0, pltpu.roll(value, 1, 0)).astype(BF)
    above = jnp.where(z == FZ - 1, 0.0, pltpu.roll(value, rows - 1, 0)).astype(BF)
    return below, value.astype(BF), above


def kernel(
    dims, f_ref, ew_ref, eb_ref, pw_ref, bw_hbm, bb_ref, ow_ref, dw_ref, db_ref, sel_ref, plane_ref, out_ref,
    f32s, base, taps, wm, wd, sums, enc, pooled, low, bw, halo_s, halo_r, pool_s, pool_r, low_s, low_r, bw_sem,
):
    nx, ny = dims
    ch, fx, lanes = f_ref.shape
    pairs = fx // 2
    rows = lanes
    wide = rows + 4 * FZ
    mid = rows + 2 * FZ
    ix, iy = lax.axis_index("sx"), lax.axis_index("sy")
    face = 2 * ny

    def there(d, e):
        ok = None
        for cond in ((ix > 0) if d < 0 else (ix < nx - 1) if d > 0 else None, (iy > 0) if e < 0 else (iy < ny - 1) if e > 0 else None):
            if cond is not None:
                ok = cond if ok is None else ok & cond
        return ok

    def partner(d, p):
        ok = there(d, 0)
        return (iy != p) if ok is None else ok

    weights = pltpu.make_async_copy(bw_hbm, bw, bw_sem)
    weights.start()

    barrier = pltpu.get_barrier_semaphore()
    for d in SIDES:
        for p in range(ny):
            @pl.when(partner(d, p))
            def _():
                pl.semaphore_signal(barrier, inc=1, device_id=(ix + d, p), device_id_type=MESH)

    f32s[...] = f_ref[...].astype(F32).reshape(ch * fx, lanes)
    for k in range(pairs):
        two = [f32s[pl.ds(2 * k + j, ch, stride=fx), :] for j in range(2)]
        base[k + 1, pl.ds(2 * FZ, rows), :] = jnp.concatenate(two, axis=0).T.astype(BF)

    present = (ix > 0).astype(jnp.int32) + (ix < nx - 1).astype(jnp.int32)
    pl.semaphore_wait(barrier, present * ny + ny - 1)

    def halo(d, e):
        src_k = pl.ds(1, pairs) if d == 0 else pl.ds(1 if d < 0 else pairs, 1)
        dst_k = pl.ds(1, pairs) if d == 0 else pl.ds(pairs + 1 if d < 0 else 0, 1)
        src_r = pl.ds(2 * FZ, rows) if e == 0 else pl.ds(2 * FZ if e < 0 else rows, 2 * FZ)
        dst_r = pl.ds(2 * FZ, rows) if e == 0 else pl.ds(rows + 2 * FZ if e < 0 else 0, 2 * FZ)
        n = (d + 1) * 3 + e + 1
        return pltpu.make_async_remote_copy(
            base.at[src_k, src_r], base.at[dst_k, dst_r], halo_s.at[n], halo_r.at[n],
            device_id=(ix + d, iy + e), device_id_type=MESH,
        )

    around = [(d, e) for d in SIDES for e in SIDES if d or e]
    for d, e in sorted(around, key=lambda de: (de[1] == 0, de[0] != 0)):
        @pl.when(there(d, e))
        def _():
            halo(d, e).start()

    arrange(ew_ref, wm)
    zeros_x = jnp.zeros((1, rows, 2 * ch), BF)
    zeros_y = jnp.zeros((pairs + 2, 2 * FZ, 2 * ch), BF)

    @pl.when(ix == 0)
    def _():
        base[pl.ds(0, 1), pl.ds(2 * FZ, rows), :] = zeros_x
        base[pl.ds(0, 1), pl.ds(0, 2 * FZ), :] = zeros_y[:1]
        base[pl.ds(0, 1), pl.ds(rows + 2 * FZ, 2 * FZ), :] = zeros_y[:1]
        pooled[0] = jnp.zeros(pooled.shape[1:], BF)

    @pl.when(ix == nx - 1)
    def _():
        base[pl.ds(pairs + 1, 1), pl.ds(2 * FZ, rows), :] = zeros_x
        base[pl.ds(pairs + 1, 1), pl.ds(0, 2 * FZ), :] = zeros_y[:1]
        base[pl.ds(pairs + 1, 1), pl.ds(rows + 2 * FZ, 2 * FZ), :] = zeros_y[:1]
        pooled[2] = jnp.zeros(pooled.shape[1:], BF)

    @pl.when(iy == 0)
    def _():
        base[:, pl.ds(0, 2 * FZ), :] = zeros_y

    @pl.when(iy == ny - 1)
    def _():
        base[:, pl.ds(rows + 2 * FZ, 2 * FZ), :] = zeros_y

    arrange(dw_ref, wd)

    for d, e in around:
        @pl.when(there(-d, -e))
        def _():
            halo(d, e).wait_recv()

    z_wide = lax.broadcasted_iota(jnp.int32, (wide, 2 * ch), 0) % FZ
    z_mid = lax.broadcasted_iota(jnp.int32, (mid, 2 * ch), 0) % FZ

    def encode(k, _):
        m, b, p = z_taps(base[k].astype(F32), z_wide)
        cols = [v[t * FZ : t * FZ + mid] for t in range(3) for v in (m, b, p)]
        sums[k] = dot_nt(jnp.concatenate(cols, axis=1), wm[...])
        return 0

    lax.fori_loop(0, pairs + 2, encode, 0)

    even = lax.broadcasted_iota(jnp.int32, (1, 2 * ch), 1) < ch

    def combine(k, count):
        tile = pl.ds(2 * ch, 2 * ch)
        before = sums[max(k - 1, 0), pl.ds(0, count), tile]
        after = sums[min(k + 1, pairs + 1), pl.ds(0, count), tile]
        return sums[k, pl.ds(0, count), pl.ds(0, 2 * ch)] + jnp.where(even, before, after)

    enc_bias = jnp.concatenate([eb_ref[...]] * 2, axis=1)
    best = []
    for k in list(range(1, pairs + 1)) + [0, pairs + 1]:
        value = jnp.maximum(combine(k, mid) + enc_bias, 0.0).astype(BF)
        enc[k] = value
        if 1 <= k <= pairs:
            own = value[FZ : FZ + rows].astype(F32).reshape(rows // FZ, 2, POOL, 2 * ch)
            own = jnp.max(own, axis=0)
            if (k - 1) % (POOL // 2) == 0:
                best.append(own)
            else:
                best[-1] = jnp.maximum(best[-1], own)
        if k == pairs:
            cells = [jnp.max(v, axis=1) for v in best]
            cells = jnp.concatenate(cells + [jnp.zeros((16 - 2 * len(cells), 2 * ch), F32)], axis=0)
            cells = jnp.maximum(cells, pltpu.roll(cells, ch, 1))
            pooled[1, iy] = cells.astype(BF)

            def pool_copy(d, p):
                return pltpu.make_async_remote_copy(
                    pooled.at[1, iy], pooled.at[1 - d, iy], pool_s.at[d + 1, p], pool_r.at[1 - d, iy],
                    device_id=(ix + d, p), device_id_type=MESH,
                )

            for d in (-1, 1, 0):
                for p in range(ny):
                    @pl.when(partner(d, p))
                    def _():
                        pool_copy(d, p).start()

    def pool_arrival(d, p):
        return pltpu.make_async_remote_copy(
            pooled.at[1, iy], pooled.at[d + 1, p], pool_s.at[d + 1, p], pool_r.at[d + 1, p],
            device_id=(ix + d, p), device_id_type=MESH,
        )

    weights.wait()
    for d in SIDES:
        for p in range(ny):
            @pl.when(partner(d, p))
            def _():
                pool_arrival(d, p).wait_recv()

    outs = 4 * ny
    cells = pooled[...].reshape(3 * ny * 16, 2 * ch)
    picked = dot(sel_ref[...], cells).astype(BF)[:, :ch]
    projected = dot(picked, pw_ref[...]).astype(BF)
    total = None
    for tap in range(27):
        term = dot_nt(projected[tap * outs : (tap + 1) * outs], bw[tap])
        total = term if total is None else total + term
    bottleneck = jnp.maximum(total + bb_ref[...], 0.0).astype(BF)
    share = dot(bottleneck, ow_ref[...])
    low[iy, 1:3] = jnp.concatenate([share, share], axis=1).reshape(2, face, 2 * ch)

    def low_copy(d, p, sender, receiver):
        src = pl.ds(1, 2) if d == 0 else pl.ds(1 if d < 0 else 2, 1)
        dst = pl.ds(1, 2) if d == 0 else pl.ds(3 if d < 0 else 0, 1)
        return pltpu.make_async_remote_copy(
            low.at[iy, src], low.at[sender, dst], low_s.at[d + 1, p], low_r.at[d + 1, receiver],
            device_id=(ix + d, p), device_id_type=MESH,
        )

    for d in (-1, 1, 0):
        for p in range(ny):
            @pl.when(partner(d, p))
            def _():
                low_copy(d, p, iy, iy).start()

    for d in SIDES:
        for p in range(ny):
            @pl.when(partner(-d, p))
            def _():
                low_copy(d, p, p, p).wait_recv()

    lowres = low[0]
    for s in range(1, ny):
        lowres = lowres + low[s]
    slots = [lowres[n] for n in range(4)]
    slots[0] = jnp.where(ix > 0, slots[0], slots[1])
    slots[3] = jnp.where(ix < nx - 1, slots[3], slots[2])
    rest = jnp.concatenate(slots, axis=1)
    parts = []
    for _ in range(3):
        part = rest.astype(BF).astype(F32)
        parts.append(part)
        rest = rest - part
    planes = dot(plane_ref[iy], jnp.concatenate(parts, axis=0).astype(BF))

    y_index = lax.broadcasted_iota(jnp.int32, (mid, 2 * ch), 0) // FZ
    inside = ((y_index > 0) | (iy > 0)) & ((y_index < rows // FZ + 1) | (iy < ny - 1))
    for k in range(pairs + 2):
        x = 2 * k - 2
        lo = (2 * x - 7) // (2 * POOL)
        w0, w1 = ((2 * (x + j) - 7 - 2 * POOL * lo) / (2 * POOL) for j in range(2))
        weight = jnp.where(even, F32(w0), F32(w1))
        first = planes[:, (lo + 1) * 2 * ch : (lo + 2) * 2 * ch]
        second = planes[:, (lo + 2) * 2 * ch : (lo + 3) * 2 * ch]
        up = (1.0 - weight) * first + weight * second
        joined = (enc[k].astype(F32) + up).astype(BF).astype(F32)
        keep = inside & (ix > 0) if k == 0 else inside & (ix < nx - 1) if k == pairs + 1 else inside
        m, b, p = z_taps(jnp.where(keep, joined, 0.0), z_mid)
        for t, v in enumerate((m, b, p)):
            taps[k, :, t * 2 * ch : (t + 1) * 2 * ch] = v

    def decode(k, _):
        cols = [taps[k, pl.ds(t * FZ, rows), :] for t in range(3)]
        sums[k, pl.ds(0, rows), :] = dot_nt(jnp.concatenate(cols, axis=1), wd[...])
        return 0

    lax.fori_loop(0, pairs + 2, decode, 0)

    dec_bias = jnp.concatenate([db_ref[...]] * 2, axis=1)
    for k in range(1, pairs + 1):
        value = (combine(k, rows) + dec_bias).T
        for j in range(2):
            f32s[pl.ds(2 * (k - 1) + j, ch, stride=fx), :] = value[j * ch : (j + 1) * ch]
    out_ref[...] = f32s[...].astype(BF).reshape(ch, fx, lanes)

    for d, e in around:
        @pl.when(there(d, e))
        def _():
            halo(d, e).wait_send()
    for d in SIDES:
        for p in range(ny):
            @pl.when(partner(d, p))
            def _():
                pool_arrival(d, p).wait_send()
                low_copy(d, p, iy, iy).wait_send()


def per_device(features, enc_weight, enc_bias, proj_weight, bottle_weight, bottle_bias, out_weight, dec_weight, dec_bias):
    channels, fine_x, merged = features.shape
    fine_y = merged // FZ
    if fine_x != 2 * POOL or fine_y != POOL:
        raise ValueError("block size")
    nx, ny = lax.axis_size("sx"), lax.axis_size("sy")
    filters, bottle = bottle_weight.shape[3:]
    pairs = fine_x // 2
    wide, mid = merged + 4 * FZ, merged + 2 * FZ
    c2 = 2 * channels
    vmem = pl.BlockSpec(memory_space=pltpu.VMEM)
    hbm = pl.BlockSpec(memory_space=pl.ANY)
    dma = pltpu.SemaphoreType.DMA
    return pl.pallas_call(
        functools.partial(kernel, (nx, ny)),
        out_shape=jax.ShapeDtypeStruct(features.shape, BF),
        in_specs=[vmem, vmem, vmem, vmem, hbm, vmem, vmem, vmem, vmem, vmem, vmem],
        out_specs=vmem,
        scratch_shapes=[
            pltpu.VMEM((channels * fine_x, merged), F32),
            pltpu.VMEM((pairs + 2, wide, c2), BF),
            pltpu.VMEM((pairs + 2, mid, 3 * c2), BF),
            pltpu.VMEM((2 * c2, 9 * c2), BF),
            pltpu.VMEM((2 * c2, 9 * c2), BF),
            pltpu.VMEM((pairs + 2, mid, 2 * c2), F32),
            pltpu.VMEM((pairs + 2, mid, c2), BF),
            pltpu.VMEM((3, ny, 16, c2), BF),
            pltpu.VMEM((ny, 4, 2 * ny, c2), F32),
            pltpu.VMEM((27, filters, bottle), BF),
            dma((9,)), dma((9,)), dma((3, ny)), dma((3, ny)), dma((3, ny)), dma((3, ny)), dma,
        ],
        compiler_params=pltpu.CompilerParams(
            collective_id=0, has_side_effects=True, vmem_limit_bytes=48 * 1024 * 1024
        ),
    )(
        features,
        enc_weight.reshape(27, channels, channels),
        enc_bias.reshape(1, channels),
        proj_weight,
        bottle_weight.reshape(27, filters, bottle),
        bottle_bias.reshape(1, filters),
        out_weight,
        dec_weight.reshape(27, channels, channels),
        dec_bias.reshape(1, channels),
        jnp.asarray(cell_selector(ny), BF),
        jnp.asarray(plane_weights(ny, fine_y), BF),
    )


def solution(mesh):
    in_specs = (
        P(None, "sx", "sy"), P(), P(), P(), P(None, None, None, "sy", None), P("sy"), P("sy", None), P(), P(),
    )
    return jax.shard_map(
        per_device, mesh=mesh, in_specs=in_specs, out_specs=P(None, "sx", "sy"), check_vma=False
    )
```

```python
import functools

import jax
import jax.numpy as jnp
import numpy as np
from jax import lax
from jax.experimental import pallas as pl
from jax.experimental.pallas import tpu as pltpu
from jax.sharding import PartitionSpec as P

POOL = 8
FZ = 16
MESH = pl.DeviceIdType.MESH
BF = jnp.bfloat16
F32 = jnp.float32
SIDES = (-1, 0, 1)


def cell_selector(y_devices):
    outs = 4 * y_devices
    sel = np.zeros((27, outs, 3 * y_devices * 16), np.float32)
    for tap in range(27):
        a, b, c = tap // 9, tap // 3 % 3, tap % 3
        for row in range(outs):
            x, y, z = row // (2 * y_devices) + a - 1, row // 2 % y_devices + b - 1, row % 2 + c - 1
            if 0 <= y < y_devices and 0 <= z < 2:
                side, slot = ((0, 1), (1, 0), (1, 1), (2, 0))[x + 1]
                sel[tap, row, (side * y_devices + y) * 16 + slot * 2 + z] = 1
    return sel.reshape(27 * outs, -1)


def row_of(g, n):
    row = np.zeros(n)
    u = min(max((2 * g - 7) / 16, 0), n - 1)
    lo = int(np.floor(u))
    row[lo] += 1 - (u - lo)
    if lo + 1 < n:
        row[lo + 1] += u - lo
    return row


def plane_weights(y_devices, fine_y):
    total = y_devices * fine_y
    table = np.zeros((y_devices, fine_y + 2, FZ, y_devices, 2), np.float32)
    for s in range(y_devices):
        for y in range(fine_y + 2):
            g = min(max(s * fine_y + y - 1, 0), total - 1)
            table[s, y] = row_of(g, y_devices)[None, :, None] * np.stack([row_of(z, 2) for z in range(FZ)])[:, None, :]
    table = table.reshape(y_devices, (fine_y + 2) * FZ, -1)
    return np.concatenate([table] * 3, axis=2)


def dot_nt(a, b):
    return lax.dot_general(a, b, (((1,), (1,)), ((), ())), preferred_element_type=F32)


def dot(a, b):
    return jnp.dot(a, b, preferred_element_type=F32)


def arrange(w_ref, wm):
    ch = w_ref.shape[1]
    zero = jnp.zeros((ch, ch), BF)
    for bc in range(9):
        w0, w1, w2 = (w_ref[a * 9 + bc] for a in range(3))
        cols = pl.ds(bc * 2 * ch, 2 * ch)
        for n, (left, right) in enumerate(((w1, w2), (w0, w1), (zero, w0), (w2, zero))):
            wm[pl.ds(n * ch, ch), cols] = jnp.concatenate([left, right], axis=1)


def z_taps(value, z):
    rows = value.shape[0]
    below = jnp.where(z == 0, 0.0, pltpu.roll(value, 1, 0)).astype(BF)
    above = jnp.where(z == FZ - 1, 0.0, pltpu.roll(value, rows - 1, 0)).astype(BF)
    return below, value.astype(BF), above


def kernel(
    dims, f_hbm, ew_hbm, eb_ref, pw_hbm, bw_hbm, bb_ref, ow_hbm, dw_hbm, db_ref, sel_hbm, plane_hbm, out_ref,
    f32s, base, taps, wm, wd, sums, enc, pooled, low, f_ref, ew_ref, dw_ref, sel_ref, plane_ref, pw_ref, ow_ref, bw,
    halo_s, halo_r, pool_s, pool_r, low_s, low_r, load_sem,
):
    nx, ny = dims
    ch, fx, lanes = f_ref.shape
    pairs = fx // 2
    rows = lanes
    wide = rows + 4 * FZ
    mid = rows + 2 * FZ
    ix, iy = lax.axis_index("sx"), lax.axis_index("sy")
    face = 2 * ny

    def there(d, e):
        ok = None
        for cond in ((ix > 0) if d < 0 else (ix < nx - 1) if d > 0 else None, (iy > 0) if e < 0 else (iy < ny - 1) if e > 0 else None):
            if cond is not None:
                ok = cond if ok is None else ok & cond
        return ok

    def partner(d, p):
        ok = there(d, 0)
        return (iy != p) if ok is None else ok

    loads = [
        pltpu.make_async_copy(src, dst, load_sem.at[n])
        for n, (src, dst) in enumerate((
            (f_hbm, f_ref), (ew_hbm, ew_ref), (dw_hbm, dw_ref), (sel_hbm, sel_ref),
            (pw_hbm, pw_ref), (ow_hbm, ow_ref), (plane_hbm, plane_ref), (bw_hbm, bw),
        ))
    ]
    for load in loads:
        load.start()

    barrier = pltpu.get_barrier_semaphore()
    for d in SIDES:
        for p in range(ny):
            @pl.when(partner(d, p))
            def _():
                pl.semaphore_signal(barrier, inc=1, device_id=(ix + d, p), device_id_type=MESH)

    loads[0].wait()
    f32s[...] = f_ref[...].astype(F32).reshape(ch * fx, lanes)
    for k in range(pairs):
        two = [f32s[pl.ds(2 * k + j, ch, stride=fx), :] for j in range(2)]
        base[k + 1, pl.ds(2 * FZ, rows), :] = jnp.concatenate(two, axis=0).T.astype(BF)

    present = (ix > 0).astype(jnp.int32) + (ix < nx - 1).astype(jnp.int32)
    pl.semaphore_wait(barrier, present * ny + ny - 1)

    def halo(d, e):
        src_k = pl.ds(1, pairs) if d == 0 else pl.ds(1 if d < 0 else pairs, 1)
        dst_k = pl.ds(1, pairs) if d == 0 else pl.ds(pairs + 1 if d < 0 else 0, 1)
        src_r = pl.ds(2 * FZ, rows) if e == 0 else pl.ds(2 * FZ if e < 0 else rows, 2 * FZ)
        dst_r = pl.ds(2 * FZ, rows) if e == 0 else pl.ds(rows + 2 * FZ if e < 0 else 0, 2 * FZ)
        n = (d + 1) * 3 + e + 1
        return pltpu.make_async_remote_copy(
            base.at[src_k, src_r], base.at[dst_k, dst_r], halo_s.at[n], halo_r.at[n],
            device_id=(ix + d, iy + e), device_id_type=MESH,
        )

    around = [(d, e) for d in SIDES for e in SIDES if d or e]
    for d, e in sorted(around, key=lambda de: (de[1] == 0, de[0] != 0)):
        @pl.when(there(d, e))
        def _():
            halo(d, e).start()

    loads[1].wait()
    arrange(ew_ref, wm)
    zeros_x = jnp.zeros((1, rows, 2 * ch), BF)
    zeros_y = jnp.zeros((pairs + 2, 2 * FZ, 2 * ch), BF)

    @pl.when(ix == 0)
    def _():
        base[pl.ds(0, 1), pl.ds(2 * FZ, rows), :] = zeros_x
        base[pl.ds(0, 1), pl.ds(0, 2 * FZ), :] = zeros_y[:1]
        base[pl.ds(0, 1), pl.ds(rows + 2 * FZ, 2 * FZ), :] = zeros_y[:1]
        pooled[0] = jnp.zeros(pooled.shape[1:], BF)

    @pl.when(ix == nx - 1)
    def _():
        base[pl.ds(pairs + 1, 1), pl.ds(2 * FZ, rows), :] = zeros_x
        base[pl.ds(pairs + 1, 1), pl.ds(0, 2 * FZ), :] = zeros_y[:1]
        base[pl.ds(pairs + 1, 1), pl.ds(rows + 2 * FZ, 2 * FZ), :] = zeros_y[:1]
        pooled[2] = jnp.zeros(pooled.shape[1:], BF)

    @pl.when(iy == 0)
    def _():
        base[:, pl.ds(0, 2 * FZ), :] = zeros_y

    @pl.when(iy == ny - 1)
    def _():
        base[:, pl.ds(rows + 2 * FZ, 2 * FZ), :] = zeros_y

    loads[2].wait()
    arrange(dw_ref, wd)

    for d, e in around:
        @pl.when(there(-d, -e))
        def _():
            halo(d, e).wait_recv()

    z_wide = lax.broadcasted_iota(jnp.int32, (wide, 2 * ch), 0) % FZ
    z_mid = lax.broadcasted_iota(jnp.int32, (mid, 2 * ch), 0) % FZ

    def encode(k, _):
        m, b, p = z_taps(base[k].astype(F32), z_wide)
        cols = [v[t * FZ : t * FZ + mid] for t in range(3) for v in (m, b, p)]
        sums[k] = dot_nt(jnp.concatenate(cols, axis=1), wm[...])
        return 0

    lax.fori_loop(0, pairs + 2, encode, 0)

    even = lax.broadcasted_iota(jnp.int32, (1, 2 * ch), 1) < ch

    def combine(k, count):
        tile = pl.ds(2 * ch, 2 * ch)
        before = sums[max(k - 1, 0), pl.ds(0, count), tile]
        after = sums[min(k + 1, pairs + 1), pl.ds(0, count), tile]
        return sums[k, pl.ds(0, count), pl.ds(0, 2 * ch)] + jnp.where(even, before, after)

    enc_bias = jnp.concatenate([eb_ref[...]] * 2, axis=1)
    best = []
    for k in list(range(1, pairs + 1)) + [0, pairs + 1]:
        value = jnp.maximum(combine(k, mid) + enc_bias, 0.0).astype(BF)
        enc[k] = value
        if 1 <= k <= pairs:
            own = value[FZ : FZ + rows].astype(F32).reshape(rows // FZ, 2, POOL, 2 * ch)
            own = jnp.max(own, axis=0)
            if (k - 1) % (POOL // 2) == 0:
                best.append(own)
            else:
                best[-1] = jnp.maximum(best[-1], own)
        if k == pairs:
            cells = [jnp.max(v, axis=1) for v in best]
            cells = jnp.concatenate(cells + [jnp.zeros((16 - 2 * len(cells), 2 * ch), F32)], axis=0)
            cells = jnp.maximum(cells, pltpu.roll(cells, ch, 1))
            pooled[1, iy] = cells.astype(BF)

            def pool_copy(d, p):
                return pltpu.make_async_remote_copy(
                    pooled.at[1, iy], pooled.at[1 - d, iy], pool_s.at[d + 1, p], pool_r.at[1 - d, iy],
                    device_id=(ix + d, p), device_id_type=MESH,
                )

            for d in (-1, 1, 0):
                for p in range(ny):
                    @pl.when(partner(d, p))
                    def _():
                        pool_copy(d, p).start()

    def pool_arrival(d, p):
        return pltpu.make_async_remote_copy(
            pooled.at[1, iy], pooled.at[d + 1, p], pool_s.at[d + 1, p], pool_r.at[d + 1, p],
            device_id=(ix + d, p), device_id_type=MESH,
        )

    for load in loads[3:]:
        load.wait()
    for d in SIDES:
        for p in range(ny):
            @pl.when(partner(d, p))
            def _():
                pool_arrival(d, p).wait_recv()

    outs = 4 * ny
    cells = pooled[...].reshape(3 * ny * 16, 2 * ch)
    picked = dot(sel_ref[...], cells).astype(BF)[:, :ch]
    projected = dot(picked, pw_ref[...]).astype(BF)
    total = None
    for tap in range(27):
        term = dot_nt(projected[tap * outs : (tap + 1) * outs], bw[tap])
        total = term if total is None else total + term
    bottleneck = jnp.maximum(total + bb_ref[...], 0.0).astype(BF)
    share = dot_nt(bottleneck, ow_ref[...])
    low[iy, 1:3] = jnp.concatenate([share, share], axis=1).reshape(2, face, 2 * ch)

    def low_copy(d, p, sender, receiver):
        src = pl.ds(1, 2) if d == 0 else pl.ds(1 if d < 0 else 2, 1)
        dst = pl.ds(1, 2) if d == 0 else pl.ds(3 if d < 0 else 0, 1)
        return pltpu.make_async_remote_copy(
            low.at[iy, src], low.at[sender, dst], low_s.at[d + 1, p], low_r.at[d + 1, receiver],
            device_id=(ix + d, p), device_id_type=MESH,
        )

    for d in (-1, 1, 0):
        for p in range(ny):
            @pl.when(partner(d, p))
            def _():
                low_copy(d, p, iy, iy).start()

    for d in SIDES:
        for p in range(ny):
            @pl.when(partner(-d, p))
            def _():
                low_copy(d, p, p, p).wait_recv()

    lowres = low[0]
    for s in range(1, ny):
        lowres = lowres + low[s]
    slots = [lowres[n] for n in range(4)]
    slots[0] = jnp.where(ix > 0, slots[0], slots[1])
    slots[3] = jnp.where(ix < nx - 1, slots[3], slots[2])
    rest = jnp.concatenate(slots, axis=1)
    parts = []
    for _ in range(3):
        part = rest.astype(BF).astype(F32)
        parts.append(part)
        rest = rest - part
    planes = dot(plane_ref[iy], jnp.concatenate(parts, axis=0).astype(BF))

    y_index = lax.broadcasted_iota(jnp.int32, (mid, 2 * ch), 0) // FZ
    inside = ((y_index > 0) | (iy > 0)) & ((y_index < rows // FZ + 1) | (iy < ny - 1))
    for k in range(pairs + 2):
        x = 2 * k - 2
        lo = (2 * x - 7) // (2 * POOL)
        w0, w1 = ((2 * (x + j) - 7 - 2 * POOL * lo) / (2 * POOL) for j in range(2))
        weight = jnp.where(even, F32(w0), F32(w1))
        first = planes[:, (lo + 1) * 2 * ch : (lo + 2) * 2 * ch]
        second = planes[:, (lo + 2) * 2 * ch : (lo + 3) * 2 * ch]
        up = (1.0 - weight) * first + weight * second
        joined = (enc[k].astype(F32) + up).astype(BF).astype(F32)
        keep = inside & (ix > 0) if k == 0 else inside & (ix < nx - 1) if k == pairs + 1 else inside
        m, b, p = z_taps(jnp.where(keep, joined, 0.0), z_mid)
        for t, v in enumerate((m, b, p)):
            taps[k, :, t * 2 * ch : (t + 1) * 2 * ch] = v

    def decode(k, _):
        cols = [taps[k, pl.ds(t * FZ, rows), :] for t in range(3)]
        sums[k, pl.ds(0, rows), :] = dot_nt(jnp.concatenate(cols, axis=1), wd[...])
        return 0

    lax.fori_loop(0, pairs + 2, decode, 0)

    dec_bias = jnp.concatenate([db_ref[...]] * 2, axis=1)
    for k in range(1, pairs + 1):
        value = (combine(k, rows) + dec_bias).T
        for j in range(2):
            f32s[pl.ds(2 * (k - 1) + j, ch, stride=fx), :] = value[j * ch : (j + 1) * ch]
    out_ref[...] = f32s[...].astype(BF).reshape(ch, fx, lanes)

    for d, e in around:
        @pl.when(there(d, e))
        def _():
            halo(d, e).wait_send()
    for d in SIDES:
        for p in range(ny):
            @pl.when(partner(d, p))
            def _():
                pool_arrival(d, p).wait_send()
                low_copy(d, p, iy, iy).wait_send()


def per_device(features, enc_weight, enc_bias, proj_weight, bottle_weight, bottle_bias, out_weight, dec_weight, dec_bias):
    channels, fine_x, merged = features.shape
    fine_y = merged // FZ
    if fine_x != 2 * POOL or fine_y != POOL:
        raise ValueError("block size")
    nx, ny = lax.axis_size("sx"), lax.axis_size("sy")
    filters, bottle = bottle_weight.shape[3:]
    pairs = fine_x // 2
    wide, mid = merged + 4 * FZ, merged + 2 * FZ
    c2 = 2 * channels
    selector = jnp.asarray(cell_selector(ny), BF)
    planes = jnp.asarray(plane_weights(ny, fine_y), BF)
    vmem = pl.BlockSpec(memory_space=pltpu.VMEM)
    hbm = pl.BlockSpec(memory_space=pl.ANY)
    dma = pltpu.SemaphoreType.DMA
    return pl.pallas_call(
        functools.partial(kernel, (nx, ny)),
        out_shape=jax.ShapeDtypeStruct(features.shape, BF),
        in_specs=[hbm, hbm, vmem, hbm, hbm, vmem, hbm, hbm, vmem, hbm, hbm],
        out_specs=vmem,
        scratch_shapes=[
            pltpu.VMEM((channels * fine_x, merged), F32),
            pltpu.VMEM((pairs + 2, wide, c2), BF),
            pltpu.VMEM((pairs + 2, mid, 3 * c2), BF),
            pltpu.VMEM((2 * c2, 9 * c2), BF),
            pltpu.VMEM((2 * c2, 9 * c2), BF),
            pltpu.VMEM((pairs + 2, mid, 2 * c2), F32),
            pltpu.VMEM((pairs + 2, mid, c2), BF),
            pltpu.VMEM((3, ny, 16, c2), BF),
            pltpu.VMEM((ny, 4, 2 * ny, c2), F32),
            pltpu.VMEM(features.shape, BF),
            pltpu.VMEM((27, channels, channels), BF),
            pltpu.VMEM((27, channels, channels), BF),
            pltpu.VMEM(selector.shape, BF),
            pltpu.VMEM(planes.shape, BF),
            pltpu.VMEM(proj_weight.shape, BF),
            pltpu.VMEM((channels, filters), BF),
            pltpu.VMEM((27, filters, bottle), BF),
            dma((9,)), dma((9,)), dma((3, ny)), dma((3, ny)), dma((3, ny)), dma((3, ny)), dma((8,)),
        ],
        compiler_params=pltpu.CompilerParams(
            collective_id=0, has_side_effects=True, vmem_limit_bytes=63 * 1024 * 1024
        ),
    )(
        features,
        enc_weight.reshape(27, channels, channels),
        enc_bias.reshape(1, channels),
        proj_weight,
        bottle_weight.reshape(27, filters, bottle),
        bottle_bias.reshape(1, filters),
        out_weight.T,
        dec_weight.reshape(27, channels, channels),
        dec_bias.reshape(1, channels),
        selector,
        planes,
    )


def solution(mesh):
    in_specs = (
        P(None, "sx", "sy"), P(), P(), P(), P(None, None, None, "sy", None), P("sy"), P("sy", None), P(), P(),
    )
    return jax.shard_map(
        per_device, mesh=mesh, in_specs=in_specs, out_specs=P(None, "sx", "sy"), check_vma=False
    )
```

```python
import functools

import jax
import jax.numpy as jnp
import numpy as np
from jax import lax
from jax.experimental import pallas as pl
from jax.experimental.pallas import tpu as pltpu
from jax.sharding import PartitionSpec as P

POOL = 8
FZ = 16
MESH = pl.DeviceIdType.MESH
BF = jnp.bfloat16
F32 = jnp.float32
SIDES = (-1, 0, 1)


def cell_selector(y_devices):
    outs = 4 * y_devices
    sel = np.zeros((27, outs, 3 * y_devices * 16), np.float32)
    for tap in range(27):
        a, b, c = tap // 9, tap // 3 % 3, tap % 3
        for row in range(outs):
            x, y, z = row // (2 * y_devices) + a - 1, row // 2 % y_devices + b - 1, row % 2 + c - 1
            if 0 <= y < y_devices and 0 <= z < 2:
                side, slot = ((0, 1), (1, 0), (1, 1), (2, 0))[x + 1]
                sel[tap, row, (side * y_devices + y) * 16 + slot * 2 + z] = 1
    return sel.reshape(27 * outs, -1)


def row_of(g, n):
    row = np.zeros(n)
    u = min(max((2 * g - 7) / 16, 0), n - 1)
    lo = int(np.floor(u))
    row[lo] += 1 - (u - lo)
    if lo + 1 < n:
        row[lo + 1] += u - lo
    return row


def plane_weights(y_devices, fine_y):
    total = y_devices * fine_y
    table = np.zeros((y_devices, fine_y + 2, FZ, y_devices, 2), np.float32)
    for s in range(y_devices):
        for y in range(fine_y + 2):
            g = min(max(s * fine_y + y - 1, 0), total - 1)
            table[s, y] = row_of(g, y_devices)[None, :, None] * np.stack([row_of(z, 2) for z in range(FZ)])[:, None, :]
    table = table.reshape(y_devices, (fine_y + 2) * FZ, -1)
    return np.concatenate([table] * 3, axis=2)


def dot_nt(a, b):
    return lax.dot_general(a, b, (((1,), (1,)), ((), ())), preferred_element_type=F32)


def dot(a, b):
    return jnp.dot(a, b, preferred_element_type=F32)


def arrange(w_ref, wm):
    ch = w_ref.shape[1]
    zero = jnp.zeros((ch, ch), BF)
    for bc in range(9):
        w0, w1, w2 = (w_ref[a * 9 + bc] for a in range(3))
        block = [jnp.concatenate(two, axis=1) for two in ((w1, w2), (w0, w1), (zero, w0), (w2, zero))]
        block = jnp.concatenate(block, axis=0).astype(F32)
        wm[pl.ds(bc * 2 * ch, 2 * ch), :] = block.T.astype(BF)


def z_taps(value, z):
    rows = value.shape[0]
    below = jnp.where(z == 0, 0.0, pltpu.roll(value, 1, 0)).astype(BF)
    above = jnp.where(z == FZ - 1, 0.0, pltpu.roll(value, rows - 1, 0)).astype(BF)
    return below, value.astype(BF), above


def kernel(
    dims, f_hbm, ew_hbm, eb_ref, pw_hbm, bw_hbm, bb_ref, ow_hbm, dw_hbm, db_ref, sel_hbm, plane_hbm, out_ref,
    f32s, base, taps, wm, wd, sums, enc, pooled, low, f_ref, ew_ref, dw_ref, sel_ref, plane_ref, pw_ref, ow_ref, bw,
    halo_s, halo_r, pool_s, pool_r, low_s, low_r, load_sem,
):
    nx, ny = dims
    ch, fx, lanes = f_ref.shape
    pairs = fx // 2
    rows = lanes
    wide = rows + 4 * FZ
    mid = rows + 2 * FZ
    ix, iy = lax.axis_index("sx"), lax.axis_index("sy")
    face = 2 * ny

    def there(d, e):
        ok = None
        for cond in ((ix > 0) if d < 0 else (ix < nx - 1) if d > 0 else None, (iy > 0) if e < 0 else (iy < ny - 1) if e > 0 else None):
            if cond is not None:
                ok = cond if ok is None else ok & cond
        return ok

    def partner(d, p):
        ok = there(d, 0)
        return (iy != p) if ok is None else ok

    loads = [
        pltpu.make_async_copy(src, dst, load_sem.at[n])
        for n, (src, dst) in enumerate((
            (f_hbm, f_ref), (ew_hbm, ew_ref), (dw_hbm, dw_ref), (sel_hbm, sel_ref),
            (pw_hbm, pw_ref), (ow_hbm, ow_ref), (plane_hbm, plane_ref), (bw_hbm, bw),
        ))
    ]
    for load in loads:
        load.start()

    barrier = pltpu.get_barrier_semaphore()
    for d in SIDES:
        for p in range(ny):
            @pl.when(partner(d, p))
            def _():
                pl.semaphore_signal(barrier, inc=1, device_id=(ix + d, p), device_id_type=MESH)

    loads[0].wait()
    f32s[...] = f_ref[...].astype(F32).reshape(ch * fx, lanes)
    for k in range(pairs):
        two = [f32s[pl.ds(2 * k + j, ch, stride=fx), :] for j in range(2)]
        base[k + 1, pl.ds(2 * FZ, rows), :] = jnp.concatenate(two, axis=0).T.astype(BF)

    present = (ix > 0).astype(jnp.int32) + (ix < nx - 1).astype(jnp.int32)
    pl.semaphore_wait(barrier, present * ny + ny - 1)

    def halo(d, e):
        src_k = pl.ds(1, pairs) if d == 0 else pl.ds(1 if d < 0 else pairs, 1)
        dst_k = pl.ds(1, pairs) if d == 0 else pl.ds(pairs + 1 if d < 0 else 0, 1)
        src_r = pl.ds(2 * FZ, rows) if e == 0 else pl.ds(2 * FZ if e < 0 else rows, 2 * FZ)
        dst_r = pl.ds(2 * FZ, rows) if e == 0 else pl.ds(rows + 2 * FZ if e < 0 else 0, 2 * FZ)
        n = (d + 1) * 3 + e + 1
        return pltpu.make_async_remote_copy(
            base.at[src_k, src_r], base.at[dst_k, dst_r], halo_s.at[n], halo_r.at[n],
            device_id=(ix + d, iy + e), device_id_type=MESH,
        )

    around = [(d, e) for d in SIDES for e in SIDES if d or e]
    for d, e in sorted(around, key=lambda de: (de[1] == 0, de[0] != 0)):
        @pl.when(there(d, e))
        def _():
            halo(d, e).start()

    loads[1].wait()
    arrange(ew_ref, wm)
    zeros_x = jnp.zeros((1, rows, 2 * ch), BF)
    zeros_y = jnp.zeros((pairs + 2, 2 * FZ, 2 * ch), BF)

    @pl.when(ix == 0)
    def _():
        base[pl.ds(0, 1), pl.ds(2 * FZ, rows), :] = zeros_x
        base[pl.ds(0, 1), pl.ds(0, 2 * FZ), :] = zeros_y[:1]
        base[pl.ds(0, 1), pl.ds(rows + 2 * FZ, 2 * FZ), :] = zeros_y[:1]
        pooled[0] = jnp.zeros(pooled.shape[1:], BF)

    @pl.when(ix == nx - 1)
    def _():
        base[pl.ds(pairs + 1, 1), pl.ds(2 * FZ, rows), :] = zeros_x
        base[pl.ds(pairs + 1, 1), pl.ds(0, 2 * FZ), :] = zeros_y[:1]
        base[pl.ds(pairs + 1, 1), pl.ds(rows + 2 * FZ, 2 * FZ), :] = zeros_y[:1]
        pooled[2] = jnp.zeros(pooled.shape[1:], BF)

    @pl.when(iy == 0)
    def _():
        base[:, pl.ds(0, 2 * FZ), :] = zeros_y

    @pl.when(iy == ny - 1)
    def _():
        base[:, pl.ds(rows + 2 * FZ, 2 * FZ), :] = zeros_y

    loads[2].wait()
    arrange(dw_ref, wd)

    for d, e in around:
        @pl.when(there(-d, -e))
        def _():
            halo(d, e).wait_recv()

    z_wide = lax.broadcasted_iota(jnp.int32, (wide, 2 * ch), 0) % FZ
    z_mid = lax.broadcasted_iota(jnp.int32, (mid, 2 * ch), 0) % FZ

    def encode(k, _):
        m, b, p = z_taps(base[k].astype(F32), z_wide)
        cols = [v[t * FZ : t * FZ + mid] for t in range(3) for v in (m, b, p)]
        sums[k] = dot(jnp.concatenate(cols, axis=1), wm[...])
        return 0

    lax.fori_loop(0, pairs + 2, encode, 0, unroll=2)

    even = lax.broadcasted_iota(jnp.int32, (1, 2 * ch), 1) < ch

    def combine(k, count):
        tile = pl.ds(2 * ch, 2 * ch)
        before = sums[max(k - 1, 0), pl.ds(0, count), tile]
        after = sums[min(k + 1, pairs + 1), pl.ds(0, count), tile]
        return sums[k, pl.ds(0, count), pl.ds(0, 2 * ch)] + jnp.where(even, before, after)

    enc_bias = jnp.concatenate([eb_ref[...]] * 2, axis=1)
    best = []
    for k in list(range(1, pairs + 1)) + [0, pairs + 1]:
        value = jnp.maximum(combine(k, mid) + enc_bias, 0.0).astype(BF)
        enc[k] = value
        if 1 <= k <= pairs:
            own = value[FZ : FZ + rows].astype(F32).reshape(rows // FZ, 2, POOL, 2 * ch)
            own = jnp.max(own, axis=0)
            if (k - 1) % (POOL // 2) == 0:
                best.append(own)
            else:
                best[-1] = jnp.maximum(best[-1], own)
        if k == pairs:
            cells = [jnp.max(v, axis=1) for v in best]
            cells = jnp.concatenate(cells + [jnp.zeros((16 - 2 * len(cells), 2 * ch), F32)], axis=0)
            cells = jnp.maximum(cells, pltpu.roll(cells, ch, 1))
            pooled[1, iy] = cells.astype(BF)

            def pool_copy(d, p):
                return pltpu.make_async_remote_copy(
                    pooled.at[1, iy], pooled.at[1 - d, iy], pool_s.at[d + 1, p], pool_r.at[1 - d, iy],
                    device_id=(ix + d, p), device_id_type=MESH,
                )

            for d in (-1, 1, 0):
                for p in range(ny):
                    @pl.when(partner(d, p))
                    def _():
                        pool_copy(d, p).start()

    def pool_arrival(d, p):
        return pltpu.make_async_remote_copy(
            pooled.at[1, iy], pooled.at[d + 1, p], pool_s.at[d + 1, p], pool_r.at[d + 1, p],
            device_id=(ix + d, p), device_id_type=MESH,
        )

    for load in loads[3:]:
        load.wait()
    for d in SIDES:
        for p in range(ny):
            @pl.when(partner(d, p))
            def _():
                pool_arrival(d, p).wait_recv()

    outs = 4 * ny
    cells = pooled[...].reshape(3 * ny * 16, 2 * ch)
    picked = dot(sel_ref[...], cells).astype(BF)[:, :ch]
    projected = dot(picked, pw_ref[...]).astype(BF)
    total = None
    for tap in range(27):
        term = dot_nt(bw[tap], projected[tap * outs : (tap + 1) * outs])
        total = term if total is None else total + term
    bottleneck = jnp.maximum(total.T + bb_ref[...], 0.0).astype(BF)
    share = dot_nt(bottleneck, ow_ref[...])
    low[iy, 1:3] = jnp.concatenate([share, share], axis=1).reshape(2, face, 2 * ch)

    def low_copy(d, p, sender, receiver):
        src = pl.ds(1, 2) if d == 0 else pl.ds(1 if d < 0 else 2, 1)
        dst = pl.ds(1, 2) if d == 0 else pl.ds(3 if d < 0 else 0, 1)
        return pltpu.make_async_remote_copy(
            low.at[iy, src], low.at[sender, dst], low_s.at[d + 1, p], low_r.at[d + 1, receiver],
            device_id=(ix + d, p), device_id_type=MESH,
        )

    for d in (-1, 1, 0):
        for p in range(ny):
            @pl.when(partner(d, p))
            def _():
                low_copy(d, p, iy, iy).start()

    for d in SIDES:
        for p in range(ny):
            @pl.when(partner(-d, p))
            def _():
                low_copy(d, p, p, p).wait_recv()

    lowres = low[0]
    for s in range(1, ny):
        lowres = lowres + low[s]
    slots = [lowres[n] for n in range(4)]
    slots[0] = jnp.where(ix > 0, slots[0], slots[1])
    slots[3] = jnp.where(ix < nx - 1, slots[3], slots[2])
    rest = jnp.concatenate(slots, axis=1)
    parts = []
    for _ in range(3):
        part = rest.astype(BF).astype(F32)
        parts.append(part)
        rest = rest - part
    planes = dot(plane_ref[iy], jnp.concatenate(parts, axis=0).astype(BF))

    y_index = lax.broadcasted_iota(jnp.int32, (mid, 2 * ch), 0) // FZ
    inside = ((y_index > 0) | (iy > 0)) & ((y_index < rows // FZ + 1) | (iy < ny - 1))
    for k in range(pairs + 2):
        x = 2 * k - 2
        lo = (2 * x - 7) // (2 * POOL)
        w0, w1 = ((2 * (x + j) - 7 - 2 * POOL * lo) / (2 * POOL) for j in range(2))
        weight = jnp.where(even, F32(w0), F32(w1))
        first = planes[:, (lo + 1) * 2 * ch : (lo + 2) * 2 * ch]
        second = planes[:, (lo + 2) * 2 * ch : (lo + 3) * 2 * ch]
        up = (1.0 - weight) * first + weight * second
        joined = (enc[k].astype(F32) + up).astype(BF).astype(F32)
        keep = inside & (ix > 0) if k == 0 else inside & (ix < nx - 1) if k == pairs + 1 else inside
        m, b, p = z_taps(jnp.where(keep, joined, 0.0), z_mid)
        for t, v in enumerate((m, b, p)):
            taps[k, :, t * 2 * ch : (t + 1) * 2 * ch] = v

    def decode(k, _):
        cols = [taps[k, pl.ds(t * FZ, rows), :] for t in range(3)]
        sums[k, pl.ds(0, rows), :] = dot(jnp.concatenate(cols, axis=1), wd[...])
        return 0

    lax.fori_loop(0, pairs + 2, decode, 0, unroll=2)

    dec_bias = jnp.concatenate([db_ref[...]] * 2, axis=1)
    for k in range(1, pairs + 1):
        value = (combine(k, rows) + dec_bias).T
        for j in range(2):
            f32s[pl.ds(2 * (k - 1) + j, ch, stride=fx), :] = value[j * ch : (j + 1) * ch]
    out_ref[...] = f32s[...].astype(BF).reshape(ch, fx, lanes)

    for d, e in around:
        @pl.when(there(d, e))
        def _():
            halo(d, e).wait_send()
    for d in SIDES:
        for p in range(ny):
            @pl.when(partner(d, p))
            def _():
                pool_arrival(d, p).wait_send()
                low_copy(d, p, iy, iy).wait_send()


def per_device(features, enc_weight, enc_bias, proj_weight, bottle_weight, bottle_bias, out_weight, dec_weight, dec_bias):
    channels, fine_x, merged = features.shape
    fine_y = merged // FZ
    if fine_x != 2 * POOL or fine_y != POOL:
        raise ValueError("block size")
    nx, ny = lax.axis_size("sx"), lax.axis_size("sy")
    filters, bottle = bottle_weight.shape[3:]
    pairs = fine_x // 2
    wide, mid = merged + 4 * FZ, merged + 2 * FZ
    c2 = 2 * channels
    selector = jnp.asarray(cell_selector(ny), BF)
    planes = jnp.asarray(plane_weights(ny, fine_y), BF)
    vmem = pl.BlockSpec(memory_space=pltpu.VMEM)
    hbm = pl.BlockSpec(memory_space=pl.ANY)
    dma = pltpu.SemaphoreType.DMA
    return pl.pallas_call(
        functools.partial(kernel, (nx, ny)),
        out_shape=jax.ShapeDtypeStruct(features.shape, BF),
        in_specs=[hbm, hbm, vmem, hbm, hbm, vmem, hbm, hbm, vmem, hbm, hbm],
        out_specs=vmem,
        scratch_shapes=[
            pltpu.VMEM((channels * fine_x, merged), F32),
            pltpu.VMEM((pairs + 2, wide, c2), BF),
            pltpu.VMEM((pairs + 2, mid, 3 * c2), BF),
            pltpu.VMEM((9 * c2, 2 * c2), BF),
            pltpu.VMEM((9 * c2, 2 * c2), BF),
            pltpu.VMEM((pairs + 2, mid, 2 * c2), F32),
            pltpu.VMEM((pairs + 2, mid, c2), BF),
            pltpu.VMEM((3, ny, 16, c2), BF),
            pltpu.VMEM((ny, 4, 2 * ny, c2), F32),
            pltpu.VMEM(features.shape, BF),
            pltpu.VMEM((27, channels, channels), BF),
            pltpu.VMEM((27, channels, channels), BF),
            pltpu.VMEM(selector.shape, BF),
            pltpu.VMEM(planes.shape, BF),
            pltpu.VMEM(proj_weight.shape, BF),
            pltpu.VMEM((channels, filters), BF),
            pltpu.VMEM((27, filters, bottle), BF),
            dma((9,)), dma((9,)), dma((3, ny)), dma((3, ny)), dma((3, ny)), dma((3, ny)), dma((8,)),
        ],
        compiler_params=pltpu.CompilerParams(
            collective_id=0, has_side_effects=True, vmem_limit_bytes=63 * 1024 * 1024
        ),
    )(
        features,
        enc_weight.reshape(27, channels, channels),
        enc_bias.reshape(1, channels),
        proj_weight,
        bottle_weight.reshape(27, filters, bottle),
        bottle_bias.reshape(1, filters),
        out_weight.T,
        dec_weight.reshape(27, channels, channels),
        dec_bias.reshape(1, channels),
        selector,
        planes,
    )


def solution(mesh):
    in_specs = (
        P(None, "sx", "sy"), P(), P(), P(), P(None, None, None, "sy", None), P("sy"), P("sy", None), P(), P(),
    )
    return jax.shard_map(
        per_device, mesh=mesh, in_specs=in_specs, out_specs=P(None, "sx", "sy"), check_vma=False
    )
```

```python
import functools

import jax
import jax.numpy as jnp
import numpy as np
from jax import lax
from jax.experimental import pallas as pl
from jax.experimental.pallas import tpu as pltpu
from jax.sharding import PartitionSpec as P

POOL = 8
FZ = 16
MESH = pl.DeviceIdType.MESH
BF = jnp.bfloat16
F32 = jnp.float32
SIDES = (-1, 0, 1)


def cell_selector(y_devices):
    outs = 4 * y_devices
    sel = np.zeros((27, outs, 3 * y_devices * 16), np.float32)
    for tap in range(27):
        a, b, c = tap // 9, tap // 3 % 3, tap % 3
        for row in range(outs):
            x, y, z = row // (2 * y_devices) + a - 1, row // 2 % y_devices + b - 1, row % 2 + c - 1
            if 0 <= y < y_devices and 0 <= z < 2:
                side, slot = ((0, 1), (1, 0), (1, 1), (2, 0))[x + 1]
                sel[tap, row, (side * y_devices + y) * 16 + slot * 2 + z] = 1
    return sel.reshape(27 * outs, -1)


def row_of(g, n):
    row = np.zeros(n)
    u = min(max((2 * g - 7) / 16, 0), n - 1)
    lo = int(np.floor(u))
    row[lo] += 1 - (u - lo)
    if lo + 1 < n:
        row[lo + 1] += u - lo
    return row


def plane_weights(y_devices, fine_y):
    total = y_devices * fine_y
    table = np.zeros((y_devices, fine_y + 2, FZ, y_devices, 2), np.float32)
    for s in range(y_devices):
        for y in range(fine_y + 2):
            g = min(max(s * fine_y + y - 1, 0), total - 1)
            table[s, y] = row_of(g, y_devices)[None, :, None] * np.stack([row_of(z, 2) for z in range(FZ)])[:, None, :]
    table = table.reshape(y_devices, (fine_y + 2) * FZ, -1)
    return np.concatenate([table] * 3, axis=2)


def dot_nt(a, b):
    return lax.dot_general(a, b, (((1,), (1,)), ((), ())), preferred_element_type=F32)


def dot(a, b):
    return jnp.dot(a, b, preferred_element_type=F32)


def arrange(w_ref, wm):
    ch = w_ref.shape[1]
    zero = jnp.zeros((ch, ch), BF)
    for bc in range(9):
        w0, w1, w2 = (w_ref[a * 9 + bc] for a in range(3))
        block = [jnp.concatenate(two, axis=1) for two in ((w1, w2), (w0, w1), (zero, w0), (w2, zero))]
        block = jnp.concatenate(block, axis=0).astype(F32)
        wm[pl.ds(bc * 2 * ch, 2 * ch), :] = block.T.astype(BF)


def z_taps(value, z):
    rows = value.shape[0]
    below = jnp.where(z == 0, 0.0, pltpu.roll(value, 1, 0)).astype(BF)
    above = jnp.where(z == FZ - 1, 0.0, pltpu.roll(value, rows - 1, 0)).astype(BF)
    return below, value.astype(BF), above


def kernel(
    dims, f_hbm, ew_hbm, eb_ref, pw_hbm, bw_hbm, bb_ref, ow_hbm, dw_hbm, db_ref, sel_hbm, plane_hbm, out_ref,
    f32s, base, taps, wm, wd, sums, enc, pooled, low, f_ref, ew_ref, dw_ref, sel_ref, plane_ref, pw_ref, ow_ref, bw,
    halo_s, halo_r, pool_s, pool_r, low_s, low_r, load_sem,
):
    nx, ny = dims
    ch, fx, lanes = f_ref.shape
    pairs = fx // 2
    rows = lanes
    wide = rows + 4 * FZ
    mid = rows + 2 * FZ
    ix, iy = lax.axis_index("sx"), lax.axis_index("sy")
    face = 2 * ny

    def there(d, e):
        ok = None
        for cond in ((ix > 0) if d < 0 else (ix < nx - 1) if d > 0 else None, (iy > 0) if e < 0 else (iy < ny - 1) if e > 0 else None):
            if cond is not None:
                ok = cond if ok is None else ok & cond
        return ok

    def partner(d, p):
        ok = there(d, 0)
        return (iy != p) if ok is None else ok

    loads = [
        pltpu.make_async_copy(src, dst, load_sem.at[n])
        for n, (src, dst) in enumerate((
            (f_hbm, f_ref), (ew_hbm, ew_ref), (dw_hbm, dw_ref), (sel_hbm, sel_ref),
            (pw_hbm, pw_ref), (ow_hbm, ow_ref), (plane_hbm, plane_ref), (bw_hbm, bw),
        ))
    ]
    for load in loads:
        load.start()

    barrier = pltpu.get_barrier_semaphore()
    for d in SIDES:
        for p in range(ny):
            @pl.when(partner(d, p))
            def _():
                pl.semaphore_signal(barrier, inc=1, device_id=(ix + d, p), device_id_type=MESH)

    loads[0].wait()
    f32s[...] = f_ref[...].astype(F32).reshape(ch * fx, lanes)
    for k in range(pairs):
        two = [f32s[pl.ds(2 * k + j, ch, stride=fx), :] for j in range(2)]
        base[k + 1, pl.ds(2 * FZ, rows), :] = jnp.concatenate(two, axis=0).T.astype(BF)

    present = (ix > 0).astype(jnp.int32) + (ix < nx - 1).astype(jnp.int32)
    pl.semaphore_wait(barrier, present * ny + ny - 1)

    def halo(d, e):
        src_k = pl.ds(1, pairs) if d == 0 else pl.ds(1 if d < 0 else pairs, 1)
        dst_k = pl.ds(1, pairs) if d == 0 else pl.ds(pairs + 1 if d < 0 else 0, 1)
        src_r = pl.ds(2 * FZ, rows) if e == 0 else pl.ds(2 * FZ if e < 0 else rows, 2 * FZ)
        dst_r = pl.ds(2 * FZ, rows) if e == 0 else pl.ds(rows + 2 * FZ if e < 0 else 0, 2 * FZ)
        n = (d + 1) * 3 + e + 1
        return pltpu.make_async_remote_copy(
            base.at[src_k, src_r], base.at[dst_k, dst_r], halo_s.at[n], halo_r.at[n],
            device_id=(ix + d, iy + e), device_id_type=MESH,
        )

    around = [(d, e) for d in SIDES for e in SIDES if d or e]
    for d, e in sorted(around, key=lambda de: (de[1] == 0, de[0] != 0)):
        @pl.when(there(d, e))
        def _():
            halo(d, e).start()

    loads[1].wait()
    arrange(ew_ref, wm)
    zeros_x = jnp.zeros((1, rows, 2 * ch), BF)
    zeros_y = jnp.zeros((pairs + 2, 2 * FZ, 2 * ch), BF)

    @pl.when(ix == 0)
    def _():
        base[pl.ds(0, 1), pl.ds(2 * FZ, rows), :] = zeros_x
        base[pl.ds(0, 1), pl.ds(0, 2 * FZ), :] = zeros_y[:1]
        base[pl.ds(0, 1), pl.ds(rows + 2 * FZ, 2 * FZ), :] = zeros_y[:1]
        pooled[0] = jnp.zeros(pooled.shape[1:], BF)

    @pl.when(ix == nx - 1)
    def _():
        base[pl.ds(pairs + 1, 1), pl.ds(2 * FZ, rows), :] = zeros_x
        base[pl.ds(pairs + 1, 1), pl.ds(0, 2 * FZ), :] = zeros_y[:1]
        base[pl.ds(pairs + 1, 1), pl.ds(rows + 2 * FZ, 2 * FZ), :] = zeros_y[:1]
        pooled[2] = jnp.zeros(pooled.shape[1:], BF)

    @pl.when(iy == 0)
    def _():
        base[:, pl.ds(0, 2 * FZ), :] = zeros_y

    @pl.when(iy == ny - 1)
    def _():
        base[:, pl.ds(rows + 2 * FZ, 2 * FZ), :] = zeros_y

    loads[2].wait()
    arrange(dw_ref, wd)

    for d, e in around:
        @pl.when(there(-d, -e))
        def _():
            halo(d, e).wait_recv()

    z_wide = lax.broadcasted_iota(jnp.int32, (wide, 2 * ch), 0) % FZ
    z_mid = lax.broadcasted_iota(jnp.int32, (mid, 2 * ch), 0) % FZ

    group = (pairs + 2) // 2

    def encode(g, _):
        lhs = []
        for n in range(group):
            m, b, p = z_taps(base[g * group + n].astype(F32), z_wide)
            cols = [v[t * FZ : t * FZ + mid] for t in range(3) for v in (m, b, p)]
            lhs.append(jnp.concatenate(cols, axis=1))
        value = dot(jnp.concatenate(lhs, axis=0), wm[...])
        sums[pl.ds(g * group, group)] = value.reshape(group, mid, 4 * ch)
        return 0

    lax.fori_loop(0, 2, encode, 0)

    even = lax.broadcasted_iota(jnp.int32, (1, 2 * ch), 1) < ch

    def combine(k, count):
        tile = pl.ds(2 * ch, 2 * ch)
        before = sums[max(k - 1, 0), pl.ds(0, count), tile]
        after = sums[min(k + 1, pairs + 1), pl.ds(0, count), tile]
        return sums[k, pl.ds(0, count), pl.ds(0, 2 * ch)] + jnp.where(even, before, after)

    enc_bias = jnp.concatenate([eb_ref[...]] * 2, axis=1)
    best = []
    for k in list(range(1, pairs + 1)) + [0, pairs + 1]:
        value = jnp.maximum(combine(k, mid) + enc_bias, 0.0).astype(BF)
        enc[k] = value
        if 1 <= k <= pairs:
            own = value[FZ : FZ + rows].astype(F32).reshape(rows // FZ, 2, POOL, 2 * ch)
            own = jnp.max(own, axis=0)
            if (k - 1) % (POOL // 2) == 0:
                best.append(own)
            else:
                best[-1] = jnp.maximum(best[-1], own)
        if k == pairs:
            cells = [jnp.max(v, axis=1) for v in best]
            cells = jnp.concatenate(cells + [jnp.zeros((16 - 2 * len(cells), 2 * ch), F32)], axis=0)
            cells = jnp.maximum(cells, pltpu.roll(cells, ch, 1))
            pooled[1, iy] = cells.astype(BF)

            def pool_copy(d, p):
                return pltpu.make_async_remote_copy(
                    pooled.at[1, iy], pooled.at[1 - d, iy], pool_s.at[d + 1, p], pool_r.at[1 - d, iy],
                    device_id=(ix + d, p), device_id_type=MESH,
                )

            for d in (-1, 1, 0):
                for p in range(ny):
                    @pl.when(partner(d, p))
                    def _():
                        pool_copy(d, p).start()

    def pool_arrival(d, p):
        return pltpu.make_async_remote_copy(
            pooled.at[1, iy], pooled.at[d + 1, p], pool_s.at[d + 1, p], pool_r.at[d + 1, p],
            device_id=(ix + d, p), device_id_type=MESH,
        )

    for load in loads[3:]:
        load.wait()
    for d in SIDES:
        for p in range(ny):
            @pl.when(partner(d, p))
            def _():
                pool_arrival(d, p).wait_recv()

    outs = 4 * ny
    cells = pooled[...].reshape(3 * ny * 16, 2 * ch)
    picked = dot(sel_ref[...], cells).astype(BF)[:, :ch]
    projected = dot(picked, pw_ref[...]).astype(BF)
    total = None
    for tap in range(27):
        term = dot_nt(bw[tap], projected[tap * outs : (tap + 1) * outs])
        total = term if total is None else total + term
    bottleneck = jnp.maximum(total.T + bb_ref[...], 0.0).astype(BF)
    share = dot_nt(bottleneck, ow_ref[...])
    low[iy, 1:3] = jnp.concatenate([share, share], axis=1).reshape(2, face, 2 * ch)

    def low_copy(d, p, sender, receiver):
        src = pl.ds(1, 2) if d == 0 else pl.ds(1 if d < 0 else 2, 1)
        dst = pl.ds(1, 2) if d == 0 else pl.ds(3 if d < 0 else 0, 1)
        return pltpu.make_async_remote_copy(
            low.at[iy, src], low.at[sender, dst], low_s.at[d + 1, p], low_r.at[d + 1, receiver],
            device_id=(ix + d, p), device_id_type=MESH,
        )

    for d in (-1, 1, 0):
        for p in range(ny):
            @pl.when(partner(d, p))
            def _():
                low_copy(d, p, iy, iy).start()

    for d in SIDES:
        for p in range(ny):
            @pl.when(partner(-d, p))
            def _():
                low_copy(d, p, p, p).wait_recv()

    lowres = low[0]
    for s in range(1, ny):
        lowres = lowres + low[s]
    slots = [lowres[n] for n in range(4)]
    slots[0] = jnp.where(ix > 0, slots[0], slots[1])
    slots[3] = jnp.where(ix < nx - 1, slots[3], slots[2])
    rest = jnp.concatenate(slots, axis=1)
    parts = []
    for _ in range(3):
        part = rest.astype(BF).astype(F32)
        parts.append(part)
        rest = rest - part
    planes = dot(plane_ref[iy], jnp.concatenate(parts, axis=0).astype(BF))

    y_index = lax.broadcasted_iota(jnp.int32, (mid, 2 * ch), 0) // FZ
    inside = ((y_index > 0) | (iy > 0)) & ((y_index < rows // FZ + 1) | (iy < ny - 1))
    for k in range(pairs + 2):
        x = 2 * k - 2
        lo = (2 * x - 7) // (2 * POOL)
        w0, w1 = ((2 * (x + j) - 7 - 2 * POOL * lo) / (2 * POOL) for j in range(2))
        weight = jnp.where(even, F32(w0), F32(w1))
        first = planes[:, (lo + 1) * 2 * ch : (lo + 2) * 2 * ch]
        second = planes[:, (lo + 2) * 2 * ch : (lo + 3) * 2 * ch]
        up = (1.0 - weight) * first + weight * second
        joined = (enc[k].astype(F32) + up).astype(BF).astype(F32)
        keep = inside & (ix > 0) if k == 0 else inside & (ix < nx - 1) if k == pairs + 1 else inside
        m, b, p = z_taps(jnp.where(keep, joined, 0.0), z_mid)
        for t, v in enumerate((m, b, p)):
            taps[k, :, t * 2 * ch : (t + 1) * 2 * ch] = v

    def decode(g, _):
        lhs = []
        for n in range(group):
            cols = [taps[g * group + n, pl.ds(t * FZ, rows), :] for t in range(3)]
            lhs.append(jnp.concatenate(cols, axis=1))
        value = dot(jnp.concatenate(lhs, axis=0), wd[...])
        sums[pl.ds(g * group, group), pl.ds(0, rows), :] = value.reshape(group, rows, 4 * ch)
        return 0

    lax.fori_loop(0, 2, decode, 0)

    dec_bias = jnp.concatenate([db_ref[...]] * 2, axis=1)
    for k in range(1, pairs + 1):
        value = (combine(k, rows) + dec_bias).T
        for j in range(2):
            f32s[pl.ds(2 * (k - 1) + j, ch, stride=fx), :] = value[j * ch : (j + 1) * ch]
    out_ref[...] = f32s[...].astype(BF).reshape(ch, fx, lanes)

    for d, e in around:
        @pl.when(there(d, e))
        def _():
            halo(d, e).wait_send()
    for d in SIDES:
        for p in range(ny):
            @pl.when(partner(d, p))
            def _():
                pool_arrival(d, p).wait_send()
                low_copy(d, p, iy, iy).wait_send()


def per_device(features, enc_weight, enc_bias, proj_weight, bottle_weight, bottle_bias, out_weight, dec_weight, dec_bias):
    channels, fine_x, merged = features.shape
    fine_y = merged // FZ
    if fine_x != 2 * POOL or fine_y != POOL:
        raise ValueError("block size")
    nx, ny = lax.axis_size("sx"), lax.axis_size("sy")
    filters, bottle = bottle_weight.shape[3:]
    pairs = fine_x // 2
    wide, mid = merged + 4 * FZ, merged + 2 * FZ
    c2 = 2 * channels
    selector = jnp.asarray(cell_selector(ny), BF)
    planes = jnp.asarray(plane_weights(ny, fine_y), BF)
    vmem = pl.BlockSpec(memory_space=pltpu.VMEM)
    hbm = pl.BlockSpec(memory_space=pl.ANY)
    dma = pltpu.SemaphoreType.DMA
    return pl.pallas_call(
        functools.partial(kernel, (nx, ny)),
        out_shape=jax.ShapeDtypeStruct(features.shape, BF),
        in_specs=[hbm, hbm, vmem, hbm, hbm, vmem, hbm, hbm, vmem, hbm, hbm],
        out_specs=vmem,
        scratch_shapes=[
            pltpu.VMEM((channels * fine_x, merged), F32),
            pltpu.VMEM((pairs + 2, wide, c2), BF),
            pltpu.VMEM((pairs + 2, mid, 3 * c2), BF),
            pltpu.VMEM((9 * c2, 2 * c2), BF),
            pltpu.VMEM((9 * c2, 2 * c2), BF),
            pltpu.VMEM((pairs + 2, mid, 2 * c2), F32),
            pltpu.VMEM((pairs + 2, mid, c2), BF),
            pltpu.VMEM((3, ny, 16, c2), BF),
            pltpu.VMEM((ny, 4, 2 * ny, c2), F32),
            pltpu.VMEM(features.shape, BF),
            pltpu.VMEM((27, channels, channels), BF),
            pltpu.VMEM((27, channels, channels), BF),
            pltpu.VMEM(selector.shape, BF),
            pltpu.VMEM(planes.shape, BF),
            pltpu.VMEM(proj_weight.shape, BF),
            pltpu.VMEM((channels, filters), BF),
            pltpu.VMEM((27, filters, bottle), BF),
            dma((9,)), dma((9,)), dma((3, ny)), dma((3, ny)), dma((3, ny)), dma((3, ny)), dma((8,)),
        ],
        compiler_params=pltpu.CompilerParams(
            collective_id=0, has_side_effects=True, vmem_limit_bytes=63 * 1024 * 1024
        ),
    )(
        features,
        enc_weight.reshape(27, channels, channels),
        enc_bias.reshape(1, channels),
        proj_weight,
        bottle_weight.reshape(27, filters, bottle),
        bottle_bias.reshape(1, filters),
        out_weight.T,
        dec_weight.reshape(27, channels, channels),
        dec_bias.reshape(1, channels),
        selector,
        planes,
    )


def solution(mesh):
    in_specs = (
        P(None, "sx", "sy"), P(), P(), P(), P(None, None, None, "sy", None), P("sy"), P("sy", None), P(), P(),
    )
    return jax.shard_map(
        per_device, mesh=mesh, in_specs=in_specs, out_specs=P(None, "sx", "sy"), check_vma=False
    )
```
